128 devices in a mesh: row: 8 (over z, core), col: 16 (over y, x).
Axes of the slice: x: 4, y: 4, z: 4, core: 2. Of those that a mesh axis runs over, the one named last changes fastest.
Arguments:
- a_tiles: float32 [2048, 128, 128], P(('row', 'col')), may hold values from -6 to 6
- a_index: int32 [2048], P(('row', 'col')), may hold values from 0 to 4095, as said below
- d_values: float32 [4096, 8192], P('row', 'col'), may hold values from -0.1875 to 0.1875
- d_mask: int32 [32, 64], P('row', 'col'), may hold values 0 or 1
Outputs:
- contracted: float32 [16384, 8192], P('row', 'col')
The draws below stay inside these ranges and needn't reach their ends.
Inputs may be any that keep to these rules, and one draw needn't show every extreme that they name: `a_index`: the stored positions are distinct. Device s (in the order row then col) holds entries s * 16 to s * 16 + 15, and each has block row between 16 * r and 16 * r + 15, r being that device's row index. With the device at row r and column c owning block rows 16 * r to 16 * r + 15 and block columns 2 * c to 2 * c + 1, at most 2 blocks of one device are owned by one device, reached in every draw; in every row of devices one device owns 16 * 2 stored blocks and another none.
All inputs are finite; a program needn't handle non-finite values. No bound on the sum of `d_mask` on one device may be relied on, other than what follows from the above.
Results may differ from the reference program's by a relative error of at most 0.00007.
Values sent between devices are 32-bit elements; how exact they have to be, the bound alone decides.
No kernel may reach another device: no remote copies, remote signals or barrier semaphores. Data moves between devices by JAX's collectives and lax.ppermute only.
A program may use at most 320 MiB of HBM per device.

```python
from functools import partial
import jax
import jax.numpy as jnp
from jax import lax

TILE = 128
MBL = 16
KBL = 2
MB = 128
KB = 32
NB = 64
SLOTS = 16
N_ROW = 8
N_COL = 16


def shuffled(subkey, length):
    return jax.random.permutation(subkey, length)


def draw_a_index(key, part):
    key = jax.random.fold_in(key, 7)
    cell_count = MBL * KBL
    half_cells = cell_count // 2
    key_order, key_shift, key_place, key_store = jax.random.split(key, 4)
    dest_order = jax.vmap(partial(shuffled, length=N_COL))(jax.random.split(key_order, N_ROW))
    shifts = jax.random.randint(key_shift, (N_ROW, N_COL // 2), 0, half_cells + 1)
    shifts = shifts.at[:, 0].set(half_cells)
    paired = jnp.stack([half_cells + shifts, half_cells - shifts], axis=2).reshape(N_ROW, N_COL)
    row_ids = jnp.arange(N_ROW, dtype=jnp.int32)[:, None]
    counts_per = jnp.zeros((N_ROW, N_COL), jnp.int32).at[row_ids, dest_order].set(paired)
    places = jax.vmap(partial(shuffled, length=cell_count))(jax.random.split(key_place, N_ROW * N_COL))
    places = places.reshape(N_ROW, N_COL, cell_count).astype(jnp.int32)
    live = jnp.arange(cell_count, dtype=jnp.int32)[None, None, :] < counts_per[:, :, None]
    live_flat = live.reshape(N_ROW, N_COL * cell_count)
    ranking = jnp.cumsum(live_flat.astype(jnp.int32), axis=1) - 1
    col_ids = jnp.arange(N_COL, dtype=jnp.int32)[None, :, None]
    block_row = row_ids[:, :, None] * MBL + places // KBL
    block_col = col_ids * KBL + places % KBL
    values_flat = (block_row * (KBL * N_COL) + block_col).reshape(N_ROW, N_COL * cell_count)
    store_perm = jax.vmap(partial(shuffled, length=N_COL))(jax.random.split(key_store, N_ROW)).astype(jnp.int32)
    store_col = jnp.take_along_axis(store_perm, ranking % N_COL, axis=1)
    target = row_ids * (N_COL * half_cells) + store_col * half_cells + ranking // N_COL
    target = jnp.where(live_flat, target, N_ROW * N_COL * half_cells)
    result = jnp.zeros((N_ROW * N_COL * half_cells + 1,), jnp.int32).at[target.reshape(-1)].set(values_flat.reshape(-1))
    return result[:-1]


def touch_ends(values, key, smallest, largest):
    spot = [jax.random.randint(jax.random.fold_in(key, axis), (), 0, length) for axis, length in enumerate(values.shape)]
    main_axis = values.shape.index(max(values.shape))
    neighbour = spot[:main_axis] + [(spot[main_axis] + 1) % values.shape[main_axis]] + spot[main_axis + 1:]
    return values.at[tuple(spot)].set(smallest).at[tuple(neighbour)].set(largest)


def levels(stream_key, dims, pieces, low, largest):
    def one(axis_at, parts):
        draws = jax.random.uniform(jax.random.fold_in(jax.random.fold_in(stream_key, 6), axis_at), (parts,), jnp.float32, low / len(pieces), largest / len(pieces))
        return jnp.repeat(jnp.exp(draws), dims[axis_at] // parts).reshape((-1,) + (1,) * (len(dims) - axis_at - 1))

    factor_of = one(*pieces[0])
    for cut in pieces[1:]:
        factor_of = factor_of * one(*cut)
    return factor_of


def gaussian(own_key, dims, spread, limit, shards=(), held_as=jnp.bfloat16):
    array = jax.random.normal(own_key, dims, jnp.float32) * spread
    if len(shards) > 0:
        array = levels(own_key, dims, shards, -0.22, 0.18) * array
    return jnp.clip(array, min=-limit, max=limit).astype(held_as)


def setup_inputs(seed: int = 0) -> dict:
    splits = jax.random.split(jax.random.key(seed), 5)
    return {
        "a_tiles": gaussian(splits[0], (N_ROW * N_COL * SLOTS, TILE, TILE), 1.0, 6.0, ((0, 128),), jnp.float32),
        "a_index": draw_a_index(jax.random.fold_in(splits[4], 71), 0),
        "d_values": gaussian(splits[2], (KB * TILE, NB * TILE), (KB * TILE // 4) ** -0.5, 0.1875, ((0, 8), (1, 16)), jnp.float32),
        "d_mask": touch_ends((jax.random.randint(splits[3], (KB, NB), 0, 2) < 1).astype(jnp.int32), jax.random.fold_in(splits[3], 1), 0, 1),
    }


def reference(a_tiles, a_index, d_values, d_mask):
    grid_blocks = jnp.zeros((MB * KB, TILE, TILE), jnp.float32).at[a_index].set(a_tiles)
    tensor = grid_blocks.reshape(MB, KB, TILE, TILE).transpose(0, 2, 1, 3).reshape(MB * TILE, KB * TILE)
    density = (d_values.reshape(KB, TILE, NB, TILE) * d_mask.astype(jnp.float32)[:, None, :, None]).reshape(KB * TILE, NB * TILE)
    return jnp.dot(tensor, density, precision=lax.Precision.HIGHEST, preferred_element_type=jnp.float32)
```

```python
import functools

import jax
import jax.numpy as jnp
from jax import lax
from jax.experimental import pallas as pl
from jax.experimental.pallas import tpu as pltpu
from jax.sharding import Mesh, PartitionSpec as P

MBL = 16
KB = 32
NY = 4
NX = 4
HALF = 8
MARK = 8
MIB = 2**20


def ring(v, axis, n):
    perm = []
    for q, step in ((0, 1), (1, -1)):
        for i in range(n):
            at = [(j * 2 + q if axis == "z" else q * n + j) for j in (i, (i + step) % n)]
            perm.append(tuple(at))
    return lax.ppermute(v, ("z", "core") if axis == "z" else ("core", axis), perm)


def step_both(pair):
    return lax.optimization_barrier((ring(pair[0], "x", NX), ring(pair[1], "y", NY)))


def mask_kernel(mask_ref, d_ref, out_ref):
    size = out_ref.shape[0] // mask_ref.shape[0]
    for i in range(mask_ref.shape[0]):
        for j in range(mask_ref.shape[1]):
            block = slice(i * size, (i + 1) * size), slice(j * size, (j + 1) * size)
            out_ref[block] = d_ref[block] * mask_ref[i, j].astype(jnp.float32)


def mask_blocks(mask, d):
    return pl.pallas_call(
        mask_kernel,
        in_specs=[pl.BlockSpec(memory_space=pltpu.SMEM), pl.BlockSpec(memory_space=pltpu.VMEM)],
        out_specs=pl.BlockSpec(memory_space=pltpu.VMEM),
        out_shape=pltpu.VMEM(d.shape, jnp.float32),
        compiler_params=pltpu.CompilerParams(vmem_limit_bytes=8 * MIB),
        cost_estimate=pl.CostEstimate(flops=d.size, bytes_accessed=8 * d.size, transcendentals=0),
    )(mask, d)


def after(pair, others):
    return lax.optimization_barrier((*pair, *others))[: len(pair)]


def split_kernel(d_ref, hi_ref, lo_ref):
    d = d_ref[...]
    hi = d.astype(jnp.bfloat16)
    hi_ref[...] = hi
    lo_ref[...] = (d - hi.astype(jnp.float32)).astype(jnp.bfloat16)


def split(d):
    rows, width = d.shape
    block = 512
    spec = pl.BlockSpec((block, width), lambda i: (i, 0))
    return pl.pallas_call(
        split_kernel,
        grid=(rows // block,),
        in_specs=[spec],
        out_specs=[spec, spec],
        out_shape=[pltpu.VMEM(d.shape, jnp.bfloat16)] * 2,
        compiler_params=pltpu.CompilerParams(vmem_limit_bytes=8 * MIB),
        cost_estimate=pl.CostEstimate(
            flops=4 * rows * width, bytes_accessed=8 * rows * width, transcendentals=0
        ),
    )(d)


def add_kernel(marks, first, size, *refs):
    n = len(marks)
    places, sem = refs[-1 - n : -1], refs[-1]
    out = refs[-2 - n]
    if first:
        hi_ref, lo_ref, *tiles = refs[: -2 - n]
    else:
        acc, hi_ref, lo_ref, *tiles = refs[: -2 - n]
    copies = [
        pltpu.make_async_copy(t.at[pl.ds(len(m) * size, p.shape[0]), :], p, sem.at[i])
        for i, (t, m, p) in enumerate(zip(tiles, marks, places))
    ]
    for c in copies:
        c.start()
    out[...] = jnp.zeros_like(out) if first else acc[...]
    for c in copies:
        c.wait()
    todo = [(i, m) for i, mark in enumerate(marks) for m in range(len(mark))]
    group = 16 if len(todo) % 16 == 0 else 12
    for at in range(0, len(todo), group):
        products = []
        for i, m in todo[at : at + group]:
            place = places[i][marks[i][m]].astype(jnp.int32)
            k = pl.multiple_of((place & (KB - 1)) * size, size)
            t = tiles[i][m * size : (m + 1) * size, :]
            hi = t.astype(jnp.bfloat16)
            lo = (t - hi.astype(jnp.float32)).astype(jnp.bfloat16)
            dhi = hi_ref[pl.ds(k, size), :]
            dlo = lo_ref[pl.ds(k, size), :]
            product = jnp.dot(
                jnp.concatenate([hi, lo], axis=1),
                jnp.concatenate([dhi, dhi], axis=0),
                preferred_element_type=jnp.float32,
            ) + jnp.dot(hi, dlo, preferred_element_type=jnp.float32)
            products.append(((place // KB) & (MBL - 1), product))
        for r, product in products:
            out[pl.ds(pl.multiple_of(r * size, size), size), :] += product


def add_products(acc, hi, lo, tiles, marks, last=False):
    size = tiles[0].shape[1]
    depth, width = hi.shape
    first = acc is None
    vmem = pl.BlockSpec(memory_space=pltpu.VMEM)
    operands = ([] if first else [acc]) + [hi, lo, *tiles]
    total = sum(len(m) for m in marks)
    shape = (MBL * size, width)
    return pl.pallas_call(
        functools.partial(add_kernel, marks, first, size),
        in_specs=[vmem] * len(operands),
        out_specs=vmem,
        out_shape=jax.ShapeDtypeStruct(shape, jnp.float32) if last else pltpu.VMEM(shape, jnp.float32),
        input_output_aliases={} if first or last else {0: 0},
        scratch_shapes=[
            pltpu.SMEM((t.shape[0] - len(m) * size, size), jnp.float32) for t, m in zip(tiles, marks)
        ]
        + [pltpu.SemaphoreType.DMA((len(tiles),))],
        compiler_params=pltpu.CompilerParams(vmem_limit_bytes=24 * MIB),
        cost_estimate=pl.CostEstimate(
            flops=total * size * size * width * 12,
            bytes_accessed=total * size * size * 4,
            transcendentals=0,
        ),
    )(*operands)


def body(a_tiles, a_index, d_values, d_mask):
    stored, size = a_tiles.shape[0], a_tiles.shape[1]
    few = HALF // 2
    data = HALF * size
    density = lax.all_gather(mask_blocks(d_mask, d_values), ("z", "core"), axis=0, tiled=True)

    flat = a_tiles.reshape(stored * size, size)
    position = a_index.astype(jnp.float32)

    def payload(n):
        lanes = jnp.pad(position[n * HALF : (n + 1) * HALF], (0, size - HALF))
        return jnp.concatenate([flat[n * data : (n + 1) * data], jnp.broadcast_to(lanes, (MARK, size))])

    whole = [(0, j) for j in range(HALF)]

    def early(u, v):
        return jnp.concatenate([u[:data], v[: data // 2], u[data:], v[data:]])

    early_marks = whole + [(MARK, j) for j in range(few)]

    def late(u, v):
        return jnp.concatenate([u[data // 2 : data], v[:data], u[data:], v[data:]])

    late_marks = [(0, j) for j in range(few, HALF)] + [(MARK, j) for j in range(HALF)]

    a, b = payload(0), payload(1)
    p, q = [(a, b)], [(b, a)]
    for n in range(3):
        p.append(step_both(after(p[n], q[n - 1]) if n else p[n]))
        q.append(step_both(after(q[n], p[n]) if n else q[n]))
    (a1, b1), (a2, b2), (a3, b3) = p[1:]
    p4 = step_both(after((early(b1, b2), early(a1, a2)), q[2]))
    q4 = step_both(after((late(b2, b3), late(a2, a3)), q[3]))
    *p4, density = lax.optimization_barrier((*p4, density))
    *q4, density = lax.optimization_barrier((*q4, density))
    hi, lo = split(density)

    def add(acc, pairs, marks, **kw):
        tiles = [t for pair in pairs for t in pair]
        return add_products(acc, hi, lo, tiles, [m for m in marks for _ in range(2)], **kw)

    p5 = step_both(p4)
    q5 = step_both(q4)
    p6 = step_both(p5)
    q6 = step_both(q5)
    acc = add(None, [(a, b), p[1], q[1], p[2]], [whole] * 4)
    acc = add(acc, [q[2], p[3], q[3]], [whole] * 3)
    acc = add(acc, [p4, q4], [early_marks, late_marks])
    acc = add(acc, [p5, q5], [early_marks, late_marks])
    return add(acc, [p6, q6], [early_marks, late_marks], last=True)


def solution(mesh):
    grid = Mesh(mesh.devices.reshape(-1, 2, NY, NX), ("z", "core", "y", "x"))
    row, col = ("z", "core"), ("y", "x")
    in_specs = (P(row + col, None, None), P(row + col), P(row, col), P(row, col))
    return jax.shard_map(
        body, mesh=grid, in_specs=in_specs, out_specs=P(row, col), check_vma=False
    )
```

```python
import functools

import jax
import jax.numpy as jnp
from jax import lax
from jax.experimental import pallas as pl
from jax.experimental.pallas import tpu as pltpu
from jax.sharding import Mesh, PartitionSpec as P

MBL = 16
KB = 32
NY = 4
NX = 4
HALF = 8
MARK = 8
MIB = 2**20


def ring(v, axis, n):
    perm = []
    for q, step in ((0, 1), (1, -1)):
        for i in range(n):
            at = [(j * 2 + q if axis == "z" else q * n + j) for j in (i, (i + step) % n)]
            perm.append(tuple(at))
    return lax.ppermute(v, ("z", "core") if axis == "z" else ("core", axis), perm)


def step_both(pair):
    return lax.optimization_barrier((ring(pair[0], "x", NX), ring(pair[1], "y", NY)))


def prepare_kernel(index, mask, tiles_ref, d_ref, a_ref, b_ref, masked_ref, d_buf, sem):
    data = HALF * a_ref.shape[1]
    size = d_ref.shape[0] // mask.shape[0]
    copies = [
        pltpu.make_async_copy(d_ref, d_buf, sem.at[0]),
        pltpu.make_async_copy(tiles_ref.at[pl.ds(0, data), :], a_ref.at[pl.ds(0, data), :], sem.at[1]),
        pltpu.make_async_copy(tiles_ref.at[pl.ds(data, data), :], b_ref.at[pl.ds(0, data), :], sem.at[2]),
    ]
    for c in copies:
        c.start()
    lane = lax.broadcasted_iota(jnp.int32, (MARK, a_ref.shape[1]), 1)
    for n, ref in enumerate((a_ref, b_ref)):
        places = jnp.zeros(lane.shape, jnp.int32)
        for j in range(HALF):
            places = jnp.where(lane == j, index[n * HALF + j], places)
        ref[data:, :] = places.astype(jnp.float32)
    copies[0].wait()
    for i in range(mask.shape[0]):
        for j in range(mask.shape[1]):
            block = slice(i * size, (i + 1) * size), slice(j * size, (j + 1) * size)
            masked_ref[block] = d_buf[block] * mask[i, j].astype(jnp.float32)
    copies[1].wait()
    copies[2].wait()


def prepare(a_tiles, index, d, mask):
    stored, size = a_tiles.shape[0], a_tiles.shape[1]
    smem = pl.BlockSpec(memory_space=pltpu.SMEM)
    vmem = pl.BlockSpec(memory_space=pltpu.VMEM)
    payload = pltpu.VMEM((HALF * size + MARK, size), jnp.float32)
    hbm = [pltpu.with_memory_space_constraint(v, pltpu.HBM) for v in (a_tiles.reshape(stored * size, size), d)]
    return pl.pallas_call(
        prepare_kernel,
        in_specs=[smem, smem] + [pl.BlockSpec(memory_space=pltpu.HBM)] * 2,
        out_specs=[vmem] * 3,
        out_shape=[payload, payload, pltpu.VMEM(d.shape, jnp.float32)],
        scratch_shapes=[pltpu.VMEM(d.shape, jnp.float32), pltpu.SemaphoreType.DMA((3,))],
        compiler_params=pltpu.CompilerParams(vmem_limit_bytes=8 * MIB),
        cost_estimate=pl.CostEstimate(flops=d.size, bytes_accessed=16 * d.size, transcendentals=0),
    )(index, mask, *hbm)


def after(pair, others):
    return lax.optimization_barrier((*pair, *others))[: len(pair)]


def split_kernel(d_ref, hi_ref, lo_ref, d_buf, sem):
    parts = sem.shape[0]
    rows = d_ref.shape[0] // parts
    at = [pl.ds(i * rows, rows) for i in range(parts)]
    copies = [pltpu.make_async_copy(d_ref.at[r, :], d_buf.at[r, :], sem.at[i]) for i, r in enumerate(at)]
    for c in copies:
        c.start()
    for c, r in zip(copies, at):
        c.wait()
        d = d_buf[r, :]
        hi = d.astype(jnp.bfloat16)
        hi_ref[r, :] = hi
        lo_ref[r, :] = (d - hi.astype(jnp.float32)).astype(jnp.bfloat16)


def split(d):
    rows, width = d.shape
    vmem = pl.BlockSpec(memory_space=pltpu.VMEM)
    return pl.pallas_call(
        split_kernel,
        in_specs=[pl.BlockSpec(memory_space=pltpu.HBM)],
        out_specs=[vmem, vmem],
        out_shape=[pltpu.VMEM(d.shape, jnp.bfloat16)] * 2,
        scratch_shapes=[pltpu.VMEM(d.shape, jnp.float32), pltpu.SemaphoreType.DMA((8,))],
        compiler_params=pltpu.CompilerParams(vmem_limit_bytes=20 * MIB),
        cost_estimate=pl.CostEstimate(
            flops=4 * rows * width, bytes_accessed=8 * rows * width, transcendentals=0
        ),
    )(pltpu.with_memory_space_constraint(d, pltpu.HBM))


def add_kernel(marks, first, last, size, *refs):
    n = len(marks)
    operands, refs = refs[: 2 + n + (not first)], refs[2 + n + (not first) :]
    acc = None if first else operands[0]
    hi_ref, lo_ref, *tiles = operands[not first :]
    out, places, sem = refs[0], refs[1 : 1 + n], refs[1 + n]
    copies = [
        pltpu.make_async_copy(t.at[pl.ds(len(m) * size, p.shape[0]), :], p, sem.at[i])
        for i, (t, m, p) in enumerate(zip(tiles, marks, places))
    ]
    for c in copies:
        c.start()
    for c in copies:
        c.wait()
    todo = [(i, m) for i, mark in enumerate(marks) for m in range(len(mark))]
    group = 16 if len(todo) % 16 == 0 else 12

    def add_columns(out, columns):
        out[...] = jnp.zeros_like(out) if first else acc[:, columns]
        for at in range(0, len(todo), group):
            products = []
            for i, m in todo[at : at + group]:
                place = places[i][marks[i][m]].astype(jnp.int32)
                k = pl.multiple_of((place & (KB - 1)) * size, size)
                t = tiles[i][m * size : (m + 1) * size, :]
                hi = t.astype(jnp.bfloat16)
                lo = (t - hi.astype(jnp.float32)).astype(jnp.bfloat16)
                dhi = hi_ref[pl.ds(k, size), columns]
                dlo = lo_ref[pl.ds(k, size), columns]
                product = jnp.dot(
                    jnp.concatenate([hi, lo], axis=1),
                    jnp.concatenate([dhi, dhi], axis=0),
                    preferred_element_type=jnp.float32,
                ) + jnp.dot(hi, dlo, preferred_element_type=jnp.float32)
                products.append(((place // KB) & (MBL - 1), product))
            for r, product in products:
                out[pl.ds(pl.multiple_of(r * size, size), size), :] += product

    width = hi_ref.shape[1]
    if not last:
        add_columns(out, slice(0, width))
        return
    buffers, out_sem = refs[2 + n : -1], refs[-1]
    part = width // len(buffers)
    writes = []
    for h, buffer in enumerate(buffers):
        add_columns(buffer, slice(h * part, (h + 1) * part))
        write = pltpu.make_async_copy(buffer, out.at[:, pl.ds(h * part, part)], out_sem.at[h])
        write.start()
        writes.append(write)
    for write in writes:
        write.wait()


def add_products(acc, hi, lo, tiles, marks, last=False):
    size = tiles[0].shape[1]
    depth, width = hi.shape
    first = acc is None
    vmem = pl.BlockSpec(memory_space=pltpu.VMEM)
    operands = ([] if first else [acc]) + [hi, lo, *tiles]
    total = sum(len(m) for m in marks)
    shape = (MBL * size, width)
    scratch = [pltpu.SMEM((t.shape[0] - len(m) * size, size), jnp.float32) for t, m in zip(tiles, marks)]
    scratch.append(pltpu.SemaphoreType.DMA((len(tiles),)))
    if last:
        scratch += [pltpu.VMEM((shape[0], width // 2), jnp.float32)] * 2 + [pltpu.SemaphoreType.DMA((2,))]
    return pl.pallas_call(
        functools.partial(add_kernel, marks, first, last, size),
        in_specs=[vmem] * len(operands),
        out_specs=pl.BlockSpec(memory_space=pltpu.HBM) if last else vmem,
        out_shape=jax.ShapeDtypeStruct(shape, jnp.float32) if last else pltpu.VMEM(shape, jnp.float32),
        input_output_aliases={} if first or last else {0: 0},
        scratch_shapes=scratch,
        compiler_params=pltpu.CompilerParams(vmem_limit_bytes=24 * MIB),
        cost_estimate=pl.CostEstimate(
            flops=total * size * size * width * 12,
            bytes_accessed=total * size * size * 4,
            transcendentals=0,
        ),
    )(*operands)


def body(a_tiles, a_index, d_values, d_mask):
    stored, size = a_tiles.shape[0], a_tiles.shape[1]
    few = HALF // 2
    data = HALF * size
    a, b, masked = prepare(a_tiles, a_index, d_values, d_mask)
    density = lax.all_gather(masked, ("z", "core"), axis=0, tiled=True)

    whole = [(0, j) for j in range(HALF)]

    def early(u, v):
        return jnp.concatenate([u[:data], v[: data // 2], u[data:], v[data:]])

    early_marks = whole + [(MARK, j) for j in range(few)]

    def late(u, v):
        return jnp.concatenate([u[data // 2 : data], v[:data], u[data:], v[data:]])

    late_marks = [(0, j) for j in range(few, HALF)] + [(MARK, j) for j in range(HALF)]

    p1 = step_both((a, b))
    q1 = step_both((b, a))
    p2 = step_both(p1)
    q2 = step_both(after(q1, p1))
    (a1, b1), (a2, b2) = p1, p2
    p3 = after(p2, q1)
    a3, b3, u, v = lax.optimization_barrier(
        (ring(p3[0], "x", NX), ring(p3[1], "y", NY), early(b1, b2), early(a1, a2))
    )
    p3 = a3, b3
    q3 = step_both(after(q2, p2))
    p4 = step_both(after((u, v), q2))
    *p4, density, q3x, q3y = lax.optimization_barrier((*p4, density, *q3))
    q3 = q3x, q3y
    hi, lo = split(density)
    *q4, hi, lo = lax.optimization_barrier((late(b2, b3), late(a2, a3), hi, lo))
    q4 = step_both(q4)

    def add(acc, pairs, marks, **kw):
        tiles = [t for pair in pairs for t in pair]
        return add_products(acc, hi, lo, tiles, [m for m in marks for _ in range(2)], **kw)

    p5 = step_both(p4)
    q5 = step_both(q4)
    p6 = step_both(p5)
    q6 = step_both(q5)
    acc = add(None, [(a, b), p1, q1, p2], [whole] * 4)
    acc = add(acc, [q2, p3, q3], [whole] * 3)
    acc = add(acc, [p4, q4], [early_marks, late_marks])
    acc = add(acc, [p5, q5, p6], [early_marks, late_marks, early_marks])
    return add(acc, [q6], [late_marks], last=True)


def solution(mesh):
    grid = Mesh(mesh.devices.reshape(-1, 2, NY, NX), ("z", "core", "y", "x"))
    row, col = ("z", "core"), ("y", "x")
    in_specs = (P(row + col, None, None), P(row + col), P(row, col), P(row, col))
    return jax.shard_map(
        body, mesh=grid, in_specs=in_specs, out_specs=P(row, col), check_vma=False
    )
```

```python
import functools

import jax
import jax.numpy as jnp
from jax import lax
from jax.experimental import pallas as pl
from jax.experimental.pallas import tpu as pltpu
from jax.sharding import Mesh, PartitionSpec as P

MBL = 16
KB = 32
NY = 4
NX = 4
HALF = 8
MARK = 8
MIB = 2**20


def ring(v, axis, n):
    perm = []
    for q, step in ((0, 1), (1, -1)):
        for i in range(n):
            at = [(j * 2 + q if axis == "z" else q * n + j) for j in (i, (i + step) % n)]
            perm.append(tuple(at))
    return lax.ppermute(v, ("z", "core") if axis == "z" else ("core", axis), perm)


def step_both(pair):
    return lax.optimization_barrier((ring(pair[0], "x", NX), ring(pair[1], "y", NY)))


def mask_kernel(mask, d_ref, masked_ref, d_buf, sem):
    size = d_ref.shape[0] // mask.shape[0]
    rows = [pl.ds(i * size, size) for i in range(mask.shape[0])]
    copies = [pltpu.make_async_copy(d_ref.at[r, :], d_buf.at[r, :], sem.at[i]) for i, r in enumerate(rows)]
    for c in copies:
        c.start()
    for i, c in enumerate(copies):
        c.wait()
        for j in range(mask.shape[1]):
            block = slice(i * size, (i + 1) * size), slice(j * size, (j + 1) * size)
            masked_ref[block] = d_buf[block] * mask[i, j].astype(jnp.float32)


def mask_blocks(mask, d):
    return pl.pallas_call(
        mask_kernel,
        in_specs=[pl.BlockSpec(memory_space=pltpu.SMEM), pl.BlockSpec(memory_space=pltpu.HBM)],
        out_specs=pl.BlockSpec(memory_space=pltpu.VMEM),
        out_shape=pltpu.VMEM(d.shape, jnp.float32),
        scratch_shapes=[pltpu.VMEM(d.shape, jnp.float32), pltpu.SemaphoreType.DMA((mask.shape[0],))],
        compiler_params=pltpu.CompilerParams(vmem_limit_bytes=8 * MIB),
        cost_estimate=pl.CostEstimate(flops=d.size, bytes_accessed=8 * d.size, transcendentals=0),
    )(mask, pltpu.with_memory_space_constraint(d, pltpu.HBM))


def payload_kernel(index, tiles_ref, a_ref, b_ref, sem):
    data = HALF * a_ref.shape[1]
    copies = [
        pltpu.make_async_copy(tiles_ref.at[pl.ds(0, data), :], a_ref.at[pl.ds(0, data), :], sem.at[0]),
        pltpu.make_async_copy(tiles_ref.at[pl.ds(data, data), :], b_ref.at[pl.ds(0, data), :], sem.at[1]),
    ]
    for c in copies:
        c.start()
    lane = lax.broadcasted_iota(jnp.int32, (MARK, a_ref.shape[1]), 1)
    for n, ref in enumerate((a_ref, b_ref)):
        places = jnp.zeros(lane.shape, jnp.int32)
        for j in range(HALF):
            places = jnp.where(lane == j, index[n * HALF + j], places)
        ref[data:, :] = places.astype(jnp.float32)
    for c in copies:
        c.wait()


def payloads(a_tiles, index):
    stored, size = a_tiles.shape[0], a_tiles.shape[1]
    payload = pltpu.VMEM((HALF * size + MARK, size), jnp.float32)
    return pl.pallas_call(
        payload_kernel,
        in_specs=[pl.BlockSpec(memory_space=pltpu.SMEM), pl.BlockSpec(memory_space=pltpu.HBM)],
        out_specs=[pl.BlockSpec(memory_space=pltpu.VMEM)] * 2,
        out_shape=[payload, payload],
        scratch_shapes=[pltpu.SemaphoreType.DMA((2,))],
        compiler_params=pltpu.CompilerParams(vmem_limit_bytes=8 * MIB),
        cost_estimate=pl.CostEstimate(flops=0, bytes_accessed=8 * a_tiles.size, transcendentals=0),
    )(index, pltpu.with_memory_space_constraint(a_tiles.reshape(stored * size, size), pltpu.HBM))


def after(pair, others):
    return lax.optimization_barrier((*pair, *others))[: len(pair)]


def split_kernel(d_ref, hi_ref, lo_ref, d_buf, sem):
    parts = sem.shape[0]
    rows = d_ref.shape[0] // parts
    at = [pl.ds(i * rows, rows) for i in range(parts)]
    copies = [pltpu.make_async_copy(d_ref.at[r, :], d_buf.at[r, :], sem.at[i]) for i, r in enumerate(at)]
    for c in copies:
        c.start()
    for c, r in zip(copies, at):
        c.wait()
        d = d_buf[r, :]
        hi = d.astype(jnp.bfloat16)
        hi_ref[r, :] = hi
        lo_ref[r, :] = (d - hi.astype(jnp.float32)).astype(jnp.bfloat16)


def split(d):
    rows, width = d.shape
    vmem = pl.BlockSpec(memory_space=pltpu.VMEM)
    return pl.pallas_call(
        split_kernel,
        in_specs=[pl.BlockSpec(memory_space=pltpu.HBM)],
        out_specs=[vmem, vmem],
        out_shape=[pltpu.VMEM(d.shape, jnp.bfloat16)] * 2,
        scratch_shapes=[pltpu.VMEM(d.shape, jnp.float32), pltpu.SemaphoreType.DMA((8,))],
        compiler_params=pltpu.CompilerParams(vmem_limit_bytes=20 * MIB),
        cost_estimate=pl.CostEstimate(
            flops=4 * rows * width, bytes_accessed=8 * rows * width, transcendentals=0
        ),
    )(pltpu.with_memory_space_constraint(d, pltpu.HBM))


def add_kernel(marks, first, last, size, *refs):
    n = len(marks)
    operands, refs = refs[: 2 + n + (not first)], refs[2 + n + (not first) :]
    acc = None if first else operands[0]
    hi_ref, lo_ref, *tiles = operands[not first :]
    out, places, sem = refs[0], refs[1 : 1 + n], refs[1 + n]
    copies = [
        pltpu.make_async_copy(t.at[pl.ds(len(m) * size, p.shape[0]), :], p, sem.at[i])
        for i, (t, m, p) in enumerate(zip(tiles, marks, places))
    ]
    for c in copies:
        c.start()
    for c in copies:
        c.wait()
    todo = [(i, m) for i, mark in enumerate(marks) for m in range(len(mark))]
    group = 16 if len(todo) % 16 == 0 else 12

    def add_columns(out, columns):
        out[...] = jnp.zeros_like(out) if first else acc[:, columns]
        for at in range(0, len(todo), group):
            products = []
            for i, m in todo[at : at + group]:
                place = places[i][marks[i][m]].astype(jnp.int32)
                k = pl.multiple_of((place & (KB - 1)) * size, size)
                t = tiles[i][m * size : (m + 1) * size, :]
                hi = t.astype(jnp.bfloat16)
                lo = (t - hi.astype(jnp.float32)).astype(jnp.bfloat16)
                dhi = hi_ref[pl.ds(k, size), columns]
                dlo = lo_ref[pl.ds(k, size), columns]
                product = jnp.dot(
                    jnp.concatenate([hi, lo], axis=1),
                    jnp.concatenate([dhi, dhi], axis=0),
                    preferred_element_type=jnp.float32,
                ) + jnp.dot(hi, dlo, preferred_element_type=jnp.float32)
                products.append(((place // KB) & (MBL - 1), product))
            for r, product in products:
                out[pl.ds(pl.multiple_of(r * size, size), size), :] += product

    width = hi_ref.shape[1]
    if not last:
        add_columns(out, slice(0, width))
        return
    buffers, out_sem = refs[2 + n : -1], refs[-1]
    part = width // len(buffers)
    writes = []
    for h, buffer in enumerate(buffers):
        add_columns(buffer, slice(h * part, (h + 1) * part))
        write = pltpu.make_async_copy(buffer, out.at[:, pl.ds(h * part, part)], out_sem.at[h])
        write.start()
        writes.append(write)
    for write in writes:
        write.wait()


def add_products(acc, hi, lo, tiles, marks, last=False):
    size = tiles[0].shape[1]
    depth, width = hi.shape
    first = acc is None
    vmem = pl.BlockSpec(memory_space=pltpu.VMEM)
    operands = ([] if first else [acc]) + [hi, lo, *tiles]
    total = sum(len(m) for m in marks)
    shape = (MBL * size, width)
    scratch = [pltpu.SMEM((t.shape[0] - len(m) * size, size), jnp.float32) for t, m in zip(tiles, marks)]
    scratch.append(pltpu.SemaphoreType.DMA((len(tiles),)))
    if last:
        scratch += [pltpu.VMEM((shape[0], width // 2), jnp.float32)] * 2 + [pltpu.SemaphoreType.DMA((2,))]
    return pl.pallas_call(
        functools.partial(add_kernel, marks, first, last, size),
        in_specs=[vmem] * len(operands),
        out_specs=pl.BlockSpec(memory_space=pltpu.HBM) if last else vmem,
        out_shape=jax.ShapeDtypeStruct(shape, jnp.float32) if last else pltpu.VMEM(shape, jnp.float32),
        input_output_aliases={} if first or last else {0: 0},
        scratch_shapes=scratch,
        compiler_params=pltpu.CompilerParams(vmem_limit_bytes=24 * MIB),
        cost_estimate=pl.CostEstimate(
            flops=total * size * size * width * 12,
            bytes_accessed=total * size * size * 4,
            transcendentals=0,
        ),
    )(*operands)


def body(a_tiles, a_index, d_values, d_mask):
    stored, size = a_tiles.shape[0], a_tiles.shape[1]
    few = HALF // 2
    data = HALF * size
    density = lax.all_gather(mask_blocks(d_mask, d_values), ("z", "core"), axis=0, tiled=True)
    a, b = payloads(a_tiles, a_index)

    whole = [(0, j) for j in range(HALF)]

    def early(u, v):
        return jnp.concatenate([u[:data], v[: data // 2], u[data:], v[data:]])

    early_marks = whole + [(MARK, j) for j in range(few)]

    def late(u, v):
        return jnp.concatenate([u[data // 2 : data], v[:data], u[data:], v[data:]])

    late_marks = [(0, j) for j in range(few, HALF)] + [(MARK, j) for j in range(HALF)]

    p1 = step_both((a, b))
    q1 = step_both((b, a))
    p2 = step_both(p1)
    q2 = step_both(after(q1, p1))
    (a1, b1), (a2, b2) = p1, p2
    p3 = after(p2, q1)
    a3, b3, u, v = lax.optimization_barrier(
        (ring(p3[0], "x", NX), ring(p3[1], "y", NY), early(b1, b2), early(a1, a2))
    )
    p3 = a3, b3
    q3 = step_both(after(q2, p2))
    p4 = step_both(after((u, v), q2))
    *p4, density, q3x, q3y = lax.optimization_barrier((*p4, density, *q3))
    q3 = q3x, q3y
    hi, lo = split(density)
    *q4, hi, lo = lax.optimization_barrier((late(b2, b3), late(a2, a3), hi, lo))
    q4 = step_both(q4)

    def add(acc, pairs, marks, **kw):
        tiles = [t for pair in pairs for t in pair]
        return add_products(acc, hi, lo, tiles, [m for m in marks for _ in range(2)], **kw)

    p5 = step_both(p4)
    q5 = step_both(q4)
    p6 = step_both(p5)
    q6 = step_both(q5)
    acc = add(None, [(a, b), p1, q1, p2], [whole] * 4)
    acc = add(acc, [q2, p3, q3], [whole] * 3)
    acc = add(acc, [p4, q4], [early_marks, late_marks])
    acc = add(acc, [p5, q5, p6], [early_marks, late_marks, early_marks])
    return add(acc, [q6], [late_marks], last=True)


def solution(mesh):
    grid = Mesh(mesh.devices.reshape(-1, 2, NY, NX), ("z", "core", "y", "x"))
    row, col = ("z", "core"), ("y", "x")
    in_specs = (P(row + col, None, None), P(row + col), P(row, col), P(row, col))
    return jax.shard_map(
        body, mesh=grid, in_specs=in_specs, out_specs=P(row, col), check_vma=False
    )
```
